512 devices in a mesh: dp: 64 (over z, x), tensor: 8 (over y, core).
Axes of the slice: x: 4, y: 4, z: 16, core: 2. Of those that a mesh axis runs over, the one named last changes fastest.
Arguments:
- query_rows: bfloat16 [16384, 8192], P('dp', 'tensor'), may hold values from -7.5 to 7.5
- key_rows: bfloat16 [16384, 1024], P('dp', 'tensor'), may hold values from -7.5 to 7.5
- value_rows: bfloat16 [16384, 1024], P('dp', 'tensor'), may hold values from -6 to 6
- output_grad: bfloat16 [16384, 8192], P('dp', 'tensor'), may hold values from -6 to 6
- layer_input: bfloat16 [16384, 8192], P('dp', 'tensor'), may hold values from -16 to 16
- token_document: int32 [16384], P('dp'), may hold values from 0 to 255, as said below
- token_offset: int32 [16384], P('dp'), may hold values from 0 to 487, as said below
- document_server: int32 [256], replicated, may hold values from 0 to 63, as said below
Outputs:
- attended: bfloat16 [16384, 8192], P('dp', 'tensor')
- query_grad: bfloat16 [16384, 8192], P('dp', 'tensor')
- key_grad: bfloat16 [16384, 1024], P('dp', 'tensor')
- value_grad: bfloat16 [16384, 1024], P('dp', 'tensor')
- weight_grad: float32 [8192, 1024], P(('tensor', 'dp'))
The draws below stay inside these ranges and needn't reach their ends.
Inputs may be any that keep to these rules, and one draw needn't show every extreme that they name: `token_document`: token t sits on dp index t // 256. The rows of a dp index come in aligned runs of 8 rows, each run one piece of one document. At most 8 tokens of one dp index belong to the documents of one server, and in every draw some server has exactly 8 tokens from every dp index. Every document has at least one token. `token_offset`: within a piece the offsets are consecutive and rising, starting at a multiple of 8; the offsets of one document's tokens are 0 up to its length minus one, each once. `document_server`: each server is named by exactly 4 documents.
All inputs are finite; a program needn't handle non-finite values.
Results may differ from the reference program's by a relative error of at most 0.008.
The reference program's roundings to bfloat16 on the way (of `weights_low` and `grad_scores`) count: a program that leaves them out, or rounds other values in their place, can miss the bound.
Values may be sent and summed in bfloat16 or wider, within the bound.
No kernel may reach another device: no remote copies, remote signals or barrier semaphores. Data moves between devices by JAX's collectives and lax.ppermute only.
A program may use at most 64 MiB of HBM per device.

```python
import math
import jax
import jax.numpy as jnp
from jax import lax

D = 8192
QH = 64
KVH = 8
HD = 128
TOK_DEV = 256
DOCS_SRV = 4
TOKENS = 16384
CAP = 8
SLOTS = 512
NDOCS = 256
N_DP = 64


def piece_layout(key):
    keys = jax.random.split(key, 6)
    ndocs = DOCS_SRV * N_DP
    shuffled = jax.random.permutation(keys[0], ndocs).astype(jnp.int32)
    document_server = (shuffled // DOCS_SRV).astype(jnp.int32)
    inverse = jnp.zeros((ndocs,), jnp.int32).at[shuffled].set(jnp.arange(ndocs, dtype=jnp.int32))
    ranks = jnp.arange(N_DP, dtype=jnp.int32)
    half = N_DP // 2
    quarter = N_DP // 4
    amount = jax.random.randint(keys[1], (N_DP,), 0, quarter + 1).astype(jnp.int32)
    pair_amount = amount[jnp.clip((ranks - 3) // 2, 0, N_DP - 1)]
    signed = jnp.where((ranks - 3) % 2 == 0, pair_amount, -pair_amount)
    delta = jnp.where(ranks == 0, half, jnp.where(ranks < 3, -quarter, jnp.where(ranks == N_DP - 1, 0, signed)))
    server_order = jax.random.permutation(keys[2], N_DP).astype(jnp.int32)
    load = jnp.zeros((N_DP,), jnp.int32).at[server_order].set((half + delta).astype(jnp.int32))
    hottest = server_order[0]
    positions = jnp.arange(1, N_DP, dtype=jnp.int32)

    def server_cuts(cut_key, pieces):
        score = jax.random.randint(cut_key, (N_DP - 1,), 0, 1048576).astype(jnp.int32) * N_DP + positions
        score = jnp.where(positions < pieces, score, -1 - positions)
        chosen = lax.top_k(score, DOCS_SRV - 1)[0]
        return jnp.sort(chosen % N_DP).astype(jnp.int32)
    cuts = jax.vmap(server_cuts)(jax.random.split(keys[3], N_DP), load)
    fixed_cuts = jnp.arange(1, DOCS_SRV, dtype=jnp.int32)
    cuts = jnp.where((ranks == hottest)[:, None], fixed_cuts[None, :], cuts).astype(jnp.int32)
    total = N_DP * half
    piece_ids = jnp.arange(total, dtype=jnp.int32)
    server_start = (jnp.cumsum(load) - load).astype(jnp.int32)
    piece_server = (jnp.sum((server_start[None, :] <= piece_ids[:, None]).astype(jnp.int32), axis=1) - 1).astype(jnp.int32)
    within = piece_ids - server_start[piece_server]
    own_cuts = cuts[piece_server]
    part = jnp.sum((own_cuts <= within[:, None]).astype(jnp.int32), axis=1)
    earlier = jnp.take_along_axis(own_cuts, jnp.clip(part - 1, 0, DOCS_SRV - 2)[:, None], axis=1)[:, 0]
    part_begin = jnp.where(part > 0, earlier, 0)
    piece_doc = inverse[piece_server * DOCS_SRV + part]
    piece_base = ((within - part_begin) * CAP).astype(jnp.int32)
    device_perm = jax.random.permutation(keys[4], N_DP).astype(jnp.int32)

    def slot_order(slot_key):
        return jax.random.permutation(slot_key, half).astype(jnp.int32)
    slot_perm = jax.vmap(slot_order)(jax.random.split(keys[5], N_DP))
    device = device_perm[piece_ids % N_DP]
    slot = slot_perm[device, piece_ids // N_DP]
    doc_table = jnp.zeros((N_DP, half), jnp.int32).at[device, slot].set(piece_doc)
    base_table = jnp.zeros((N_DP, half), jnp.int32).at[device, slot].set(piece_base)
    within_piece = jnp.arange(CAP, dtype=jnp.int32)
    token_document = jnp.repeat(doc_table.reshape(-1), CAP).astype(jnp.int32)
    token_offset = (base_table.reshape(-1)[:, None] + within_piece[None, :]).reshape(-1).astype(jnp.int32)
    return (token_document, token_offset, document_server)


def draw_token_document(key, part):
    return piece_layout(key)[0]


def draw_token_offset(key, part):
    return piece_layout(key)[1]


def draw_document_server(key, part):
    return piece_layout(key)[2]


def draw_query_rows(key, part):
    key = jax.random.fold_in(key, 5)
    return jnp.clip(jax.random.normal(key, (TOKENS, QH * HD)), -6.0, 6.0).astype(jnp.bfloat16)


def draw_key_rows(key, part):
    key = jax.random.fold_in(key, 6)
    return jnp.clip(jax.random.normal(key, (TOKENS, KVH * HD)), -6.0, 6.0).astype(jnp.bfloat16)


def with_spikes(result, key, source, target, parts, factor):
    owner, partner = [(jnp.arange(result.shape[position]) // (result.shape[position] // parts)).reshape([-1 if axis == position else 1 for axis in range(result.ndim)]) for position in (source, target)]
    chosen = jax.random.permutation(key, parts)[partner]
    strong = (owner == chosen) | (owner == (partner + parts // 2) % parts)
    return jnp.where(strong, factor * result, result)


def block_levels(key, extent, cuts, low, top_value):
    level = 1.0
    for position, blocks in cuts:
        steps = jax.random.uniform(jax.random.fold_in(jax.random.fold_in(key, 6), position), (blocks,), jnp.float32, low / len(cuts), top_value / len(cuts))
        level = level * jnp.repeat(jnp.exp(steps), extent[position] // blocks).reshape((-1,) + (1,) * (len(extent) - 1 - position))
    return level


def normal_values(own_key, extent, width, reach, shards=(), held_as=jnp.bfloat16):
    gain = block_levels(own_key, extent, shards, -0.22, 0.18) if shards else 1.0
    entries = jax.random.normal(own_key, extent, jnp.float32) * width * gain
    return jnp.minimum(jnp.maximum(entries, -reach), reach).astype(held_as)


def bell_draw_with(own_key, dims, spread, reach, cuts, heavy, kind=jnp.bfloat16):
    values = spread * jax.random.normal(own_key, dims, jnp.float32)
    if cuts:
        values = values * block_levels(own_key, dims, cuts, -0.22, 0.18)
    return jnp.clip(with_spikes(values, jax.random.fold_in(own_key, 3), *heavy), -reach, reach).astype(kind)


def setup_inputs(seed: int = 0) -> dict:
    seeds = jax.random.split(jax.random.key(seed), 9)
    query_rows = draw_query_rows(jax.random.fold_in(seeds[8], 71), 0)
    key_rows = draw_key_rows(jax.random.fold_in(seeds[8], 71), 0)
    value_rows = normal_values(seeds[2], (TOKENS, KVH * HD), 1.0, 6.0, ((0, 64), (1, 8)))
    output_grad = normal_values(seeds[3], (TOKENS, QH * HD), 1.0, 6.0, ((0, 64), (1, 8)))
    layer_input = bell_draw_with(seeds[4], (TOKENS, D), 1.0, 16.0, ((0, 64), (1, 8)), (0, 1, 64, 4.0))
    token_document = draw_token_document(jax.random.fold_in(seeds[8], 71), 0)
    token_offset = draw_token_offset(jax.random.fold_in(seeds[8], 71), 0)
    document_server = draw_document_server(jax.random.fold_in(seeds[8], 71), 0)
    return {"query_rows": query_rows, "key_rows": key_rows, "value_rows": value_rows, "output_grad": output_grad, "layer_input": layer_input, "token_document": token_document, "token_offset": token_offset, "document_server": document_server}


NEG_FILL = -1e+30

def pick(block, index):
    return lax.dynamic_slice_in_dim(block, index * HD, HD, 1)

def add_at(block, index, part):
    return lax.dynamic_update_slice_in_dim(block, pick(block, index) + part, index * HD, 1)

def merge_heads(stacked):
    return jnp.transpose(stacked, (1, 0, 2)).reshape(stacked.shape[1], -1)

def head_scores(query_head, key_head, allowed):
    scale = float(HD) ** (-0.5)
    scores = jnp.dot(query_head, key_head.T, preferred_element_type=jnp.float32) * scale
    return jnp.where(allowed, scores, NEG_FILL)

def softmax_parts(scores):
    row_max = lax.optimization_barrier(jnp.max(scores, axis=1, keepdims=True))
    exp_scores = jnp.exp(scores - row_max)
    row_total = lax.optimization_barrier(jnp.sum(exp_scores, axis=1, keepdims=True))
    return (exp_scores / row_total, row_max, row_total)

def head_backward(weights, weights_low, row_delta, query_head, key_head, value_head, grad_head):
    scale = float(HD) ** (-0.5)
    grad_weights = jnp.dot(grad_head, value_head.T, preferred_element_type=jnp.float32)
    grad_scores = (weights * (grad_weights - row_delta)).astype(jnp.bfloat16)
    query_grad = jnp.dot(grad_scores, key_head, preferred_element_type=jnp.float32) * scale
    key_grad = jnp.dot(grad_scores.T, query_head, preferred_element_type=jnp.float32) * scale
    value_grad = jnp.dot(weights_low.T, grad_head, preferred_element_type=jnp.float32)
    return (query_grad, key_grad, value_grad)

def joint_pass(query_block, key_block, value_block, grad_block, allowed):
    slot_count = query_block.shape[0]
    query_heads = query_block.shape[1] // HD
    group = query_heads // (key_block.shape[1] // HD)

    def one_head(carry, head):
        key_acc, value_acc = carry
        kv_head = head // group
        query_head = pick(query_block, head)
        key_head = pick(key_block, kv_head)
        value_head = pick(value_block, kv_head)
        grad_head = pick(grad_block, head)
        weights, row_max, row_total = softmax_parts(head_scores(query_head, key_head, allowed))
        weights_low = weights.astype(jnp.bfloat16)
        mixed_full = jnp.dot(weights_low, value_head, preferred_element_type=jnp.float32)
        row_delta = lax.optimization_barrier(jnp.sum(grad_head.astype(jnp.float32) * mixed_full, axis=1, keepdims=True))
        query_grad, key_grad, value_grad = head_backward(weights, weights_low, row_delta, query_head, key_head, value_head, grad_head)
        key_acc = add_at(key_acc, kv_head, key_grad)
        value_acc = add_at(value_acc, kv_head, value_grad)
        return ((key_acc, value_acc), (mixed_full.astype(jnp.bfloat16), query_grad.astype(jnp.bfloat16)))
    empty = jnp.zeros((slot_count, key_block.shape[1]), jnp.float32)
    (key_acc, value_acc), (mixed, query_grad) = lax.scan(one_head, (empty, empty), jnp.arange(query_heads, dtype=jnp.int32))
    return (merge_heads(mixed), merge_heads(query_grad), key_acc.astype(jnp.bfloat16), value_acc.astype(jnp.bfloat16))

def server_layout(token_document, document_server):
    document_ids = jnp.arange(NDOCS, dtype=jnp.int32)
    match = token_document[:, None] == document_ids[None, :]
    server = lax.optimization_barrier(jnp.sum(jnp.where(match, document_server[None, :], 0), axis=1)).astype(jnp.int32)
    own_server = server.reshape(N_DP, TOK_DEV)
    member = (own_server[:, :, None] == jnp.arange(N_DP, dtype=jnp.int32)[None, None, :]).astype(jnp.int32)
    order_rank = lax.optimization_barrier(jnp.sum((jnp.cumsum(member, axis=1) - member) * member, axis=2))
    source_ids = jnp.arange(N_DP, dtype=jnp.int32)[:, None]
    flat_slot = (own_server * SLOTS + source_ids * CAP + order_rank).reshape(-1).astype(jnp.int32)
    index_table = jnp.zeros((N_DP * SLOTS,), jnp.int32).at[flat_slot].set(jnp.arange(TOKENS, dtype=jnp.int32))
    occupied_table = jnp.zeros((N_DP * SLOTS,), jnp.int32).at[flat_slot].set(1)
    return (index_table.reshape(N_DP, SLOTS), occupied_table.reshape(N_DP, SLOTS))

def reference(query_rows, key_rows, value_rows, output_grad, layer_input, token_document, token_offset, document_server):
    index_table, occupied_table = server_layout(token_document, document_server)

    def one_server(server, carry):
        attended, query_grad, key_grad, value_grad = carry
        picks = lax.dynamic_index_in_dim(index_table, server, 0, keepdims=False)
        occupied = lax.dynamic_index_in_dim(occupied_table, server, 0, keepdims=False) > 0

        def gather_rows(block):
            return jnp.where(occupied[:, None], jnp.take(block, picks, axis=0), jnp.zeros((), block.dtype))
        slot_document = jnp.where(occupied, jnp.take(token_document, picks), -1)
        slot_position = jnp.where(occupied, jnp.take(token_offset, picks), -1)
        allowed = (slot_document[:, None] == slot_document[None, :]) & (slot_position[None, :] <= slot_position[:, None])
        outputs = joint_pass(gather_rows(query_rows), gather_rows(key_rows), gather_rows(value_rows), gather_rows(output_grad), allowed)
        targets = jnp.where(occupied, picks, TOKENS)
        attended = attended.at[targets].set(outputs[0], mode='drop')
        query_grad = query_grad.at[targets].set(outputs[1], mode='drop')
        key_grad = key_grad.at[targets].set(outputs[2], mode='drop')
        value_grad = value_grad.at[targets].set(outputs[3], mode='drop')
        return (attended, query_grad, key_grad, value_grad)
    start = (jnp.zeros(query_rows.shape, jnp.bfloat16), jnp.zeros(query_rows.shape, jnp.bfloat16), jnp.zeros(key_rows.shape, jnp.bfloat16), jnp.zeros(key_rows.shape, jnp.bfloat16))
    attended, query_grad, key_grad, value_grad = lax.fori_loop(0, N_DP, one_server, start)
    weight_grad = lax.dot_general(layer_input, value_grad, (((0,), (0,)), ((), ())), preferred_element_type=jnp.float32)
    weight_grad = weight_grad * (1.0 / math.sqrt(TOKENS))
    return (attended, query_grad, key_grad, value_grad, weight_grad)
```

```python
import functools
import math

import jax
import jax.numpy as jnp
from jax import lax
from jax.experimental import pallas as pl
from jax.experimental.pallas import tpu as pltpu
from jax.sharding import Mesh
from jax.sharding import PartitionSpec as P

HD = 128
RUN = 8
X_SIZE = 4
MAX_RUNS = 64
NEG_FILL = -1e30
F32 = jnp.float32
BF16 = jnp.bfloat16
NT = (((1,), (1,)), ((), ()))
DP = ("z", "x")


def whole(memory=pltpu.VMEM):
    return pl.BlockSpec(memory_space=memory)


def params():
    return pltpu.CompilerParams(vmem_limit_bytes=50 * 1024 * 1024)


def pack_kernel(slot_ref, query_ref, grad_ref, key_ref, value_ref, out_ref):
    slots, tokens = out_ref.shape[0], slot_ref.shape[1]
    ids = lax.broadcasted_iota(jnp.int32, (slots, tokens), 0)
    hot = (ids == slot_ref[...]).astype(F32).astype(BF16)
    at = 0
    for ref in (query_ref, grad_ref, key_ref, value_ref):
        width = ref.shape[1]
        out_ref[:, at : at + width] = jnp.dot(hot, ref[...], preferred_element_type=F32).astype(BF16)
        at += width


def turn_kernel(per_z, layer_ref, out_ref):
    width = layer_ref.shape[1]
    rows = width // X_SIZE
    for x in range(X_SIZE):
        new = lax.broadcasted_iota(jnp.int32, (rows, width), 0)
        old = lax.broadcasted_iota(jnp.int32, (rows, width), 1)
        source = (new // per_z) * (per_z * X_SIZE) + x * per_z + new % per_z
        hot = (source == old).astype(F32).astype(BF16)
        out_ref[x] = lax.dot_general(hot, layer_ref[...], NT, preferred_element_type=F32).astype(BF16)


def server_kernel(group, row_doc, row_pos, col_doc, col_pos, query_ref, grad_ref, key_ref, value_ref, out_ref, bias, key_acc, value_acc):
    head = pl.program_id(0)

    @pl.when(head == 0)
    def _():
        allowed = (row_doc[...] == col_doc[...]) & (row_pos[...] <= col_pos[...])
        bias[...] = jnp.where(allowed, 0.0, NEG_FILL)
        key_acc[...] = jnp.zeros_like(key_acc)
        value_acc[...] = jnp.zeros_like(value_acc)

    scale = float(HD) ** (-0.5)
    query, grad = query_ref[...], grad_ref[...]
    scores = lax.dot_general(key_ref[...], query, NT, preferred_element_type=F32) + bias[...]
    top = jnp.max(scores, axis=0, keepdims=True)
    exp_scores = jnp.exp((scores - top) * scale)
    total = jnp.sum(exp_scores, axis=0, keepdims=True)
    weights = exp_scores * (1.0 / total)
    weights_low = weights.astype(BF16)
    grad_weights = lax.dot_general(value_ref[...], grad, NT, preferred_element_type=F32)
    row_delta = jnp.sum(weights_low.astype(F32) * grad_weights, axis=0, keepdims=True)
    grad_scores = (weights * (grad_weights - row_delta)).astype(BF16)
    value_acc[...] += jnp.dot(weights_low, grad, preferred_element_type=F32)
    key_acc[...] += jnp.dot(grad_scores, query, preferred_element_type=F32)

    @pl.when(head == group - 1)
    def _():
        out_ref[:, :HD] = (key_acc[...] * scale).astype(BF16)
        out_ref[:, HD:] = value_acc[...].astype(BF16)


def home_kernel(
    group, unroll, place_ref, reach_ref, query_ref, grad_ref, pairs_ref, mixed_ref, query_grad_ref,
    pairs, rows, query, grad, mixed, query_grad,
):
    scale = float(HD) ** (-0.5)
    count = query_ref.shape[0] // RUN
    reach_rows = rows.shape[1]
    pairs[...] = pairs_ref[...].astype(F32)
    query[...] = query_ref[...].astype(F32)
    grad[...] = grad_ref[...].astype(F32)
    rows[...] = jnp.zeros_like(rows)
    token = lax.broadcasted_iota(jnp.int32, (group * RUN, reach_rows), 0) % RUN
    other = lax.broadcasted_iota(jnp.int32, (group * RUN, reach_rows), 1)

    def stack(ref, run):
        parts = [ref[pl.ds(pl.multiple_of(run * RUN, RUN), RUN), h * HD : (h + 1) * HD] for h in range(group)]
        return jnp.concatenate(parts, axis=0)

    def unstack(ref, run, block):
        for h in range(group):
            ref[pl.ds(pl.multiple_of(run * RUN, RUN), RUN), h * HD : (h + 1) * HD] = block[h * RUN : (h + 1) * RUN]

    def step(index, carry):
        for u in range(unroll):
            run = index * unroll + u

            def bring(k, c, run=run, u=u):
                source = pl.multiple_of(place_ref[run, k] * RUN, RUN)
                rows[u, pl.ds(pl.multiple_of(k * RUN, RUN), RUN), :] = pairs[pl.ds(source, RUN), :]
                return c

            lax.fori_loop(0, reach_ref[run] + 1, bring, 0)
        for u in range(unroll):
            run = index * unroll + u
            block = rows[u].astype(BF16)
            keys, values = block[:, :HD], block[:, HD:]
            query_run = stack(query, run).astype(BF16)
            grad_full = stack(grad, run)
            grad_run = grad_full.astype(BF16)
            scores = lax.dot_general(query_run, keys, NT, preferred_element_type=F32)
            scores = jnp.where(other <= token + reach_ref[run] * RUN, scores, NEG_FILL)
            top = jnp.max(scores, axis=1, keepdims=True)
            exp_scores = jnp.exp((scores - top) * scale)
            total = jnp.sum(exp_scores, axis=1, keepdims=True)
            weights = exp_scores * (1.0 / total)
            mixed_full = jnp.dot(weights.astype(BF16), values, preferred_element_type=F32)
            row_delta = jnp.sum(grad_full * mixed_full, axis=1, keepdims=True)
            grad_weights = lax.dot_general(grad_run, values, NT, preferred_element_type=F32)
            grad_scores = (weights * (grad_weights - row_delta)).astype(BF16)
            unstack(mixed, run, mixed_full)
            unstack(query_grad, run, jnp.dot(grad_scores, keys, preferred_element_type=F32) * scale)
        return carry

    lax.fori_loop(0, count // unroll, step, 0)
    mixed_ref[...] = mixed[...].astype(BF16)
    query_grad_ref[...] = query_grad[...].astype(BF16)


def own_kernel(slot_ref, back_ref, key_grad_ref, value_grad_ref):
    slots, tokens = back_ref.shape[0], slot_ref.shape[0]
    ids = lax.broadcasted_iota(jnp.int32, (tokens, slots), 1)
    hot = (ids == slot_ref[...]).astype(F32).astype(BF16)
    rows = jnp.dot(hot, back_ref[...], preferred_element_type=F32).astype(BF16)
    key_grad_ref[...] = rows[:, :HD]
    value_grad_ref[...] = rows[:, HD:]


def weight_kernel(layer_ref, value_grad_ref, out_ref):
    for t in range(value_grad_ref.shape[0]):
        total = jnp.dot(layer_ref[0], value_grad_ref[t, 0], preferred_element_type=F32)
        for x in range(1, layer_ref.shape[0]):
            total += jnp.dot(layer_ref[x], value_grad_ref[t, x], preferred_element_type=F32)
        out_ref[:, t * HD : (t + 1) * HD] = total.astype(BF16)


def exact_pick(left, right):
    return lax.dot_general(left.astype(BF16), right.astype(BF16), NT, preferred_element_type=F32).astype(jnp.int32)


def shards(query_rows, key_rows, value_rows, output_grad, layer_input, token_document, token_offset, document_server):
    dp_size = lax.axis_size("z") * lax.axis_size("x")
    z_size = lax.axis_size("z")
    tokens = query_rows.shape[0]
    runs = tokens // RUN
    slots = dp_size * RUN
    width = query_rows.shape[1]
    group = width // HD
    me = lax.axis_index(DP)

    run_doc = token_document[::RUN]
    run_place = token_offset[::RUN] // RUN
    doc_ids = jnp.arange(document_server.shape[0], dtype=jnp.int32)
    run_server = jnp.sum(jnp.where(run_doc[:, None] == doc_ids[None, :], document_server[None, :], 0), axis=1)
    slot = (run_server[:, None] * RUN + jnp.arange(RUN, dtype=jnp.int32)[None, :]).reshape(tokens)

    sent = pl.pallas_call(
        pack_kernel,
        out_shape=jax.ShapeDtypeStruct((slots, 2 * width + 2 * HD), BF16),
        in_specs=[whole()] * 5,
        out_specs=whole(),
        compiler_params=params(),
        name="pack",
    )(slot[None, :], query_rows, output_grad, key_rows, value_rows)
    arrived = lax.all_to_all(
        sent.reshape(dp_size, RUN, -1), DP, split_axis=0, concat_axis=0, tiled=True
    ).reshape(slots, -1)

    tags = jnp.concatenate([run_doc, run_place, run_server])
    tags = jnp.pad(tags, (0, -tags.shape[0] % 128))
    all_tags = lax.all_gather(tags[None, :], DP, axis=0, tiled=True)
    all_doc, all_place, all_server = (all_tags[:, i * runs : (i + 1) * runs] for i in range(3))

    mine = all_server == me
    slot_doc = jnp.sum(jnp.where(mine, all_doc + 1, 0), axis=1) - 1
    slot_place = jnp.sum(jnp.where(mine, all_place, 0), axis=1)
    slot_doc = jnp.repeat(slot_doc, RUN)
    slot_pos = (slot_place[:, None] * RUN + jnp.arange(RUN, dtype=jnp.int32)[None, :]).reshape(slots)

    column = lambda at: pl.BlockSpec((slots, HD), lambda h, at=at: (0, at + h))
    fixed = lambda at: pl.BlockSpec((slots, HD), lambda h, at=at: (0, at))
    small = lambda shape: pl.BlockSpec(shape, lambda h: (0, 0))
    served = pl.pallas_call(
        functools.partial(server_kernel, group),
        grid=(group,),
        out_shape=jax.ShapeDtypeStruct((slots, 2 * HD), BF16),
        in_specs=[
            small((slots, 1)), small((slots, 1)), small((1, slots)), small((1, slots)),
            column(0), column(group), fixed(2 * group), fixed(2 * group + 1),
        ],
        out_specs=small((slots, 2 * HD)),
        scratch_shapes=[pltpu.VMEM((slots, slots), F32), pltpu.VMEM((slots, HD), F32), pltpu.VMEM((slots, HD), F32)],
        compiler_params=params(),
        name="server",
    )(slot_doc[:, None], slot_pos[:, None], slot_doc[None, :], slot_pos[None, :], arrived, arrived, arrived, arrived)

    back = lax.all_to_all(
        served.reshape(dp_size, RUN, -1), DP, split_axis=0, concat_axis=0, tiled=True
    ).reshape(slots, -1)
    key_grad, value_grad = pl.pallas_call(
        own_kernel,
        out_shape=[jax.ShapeDtypeStruct((tokens, HD), BF16)] * 2,
        in_specs=[whole()] * 2,
        out_specs=[whole()] * 2,
        compiler_params=params(),
        name="own",
    )(slot[:, None], back)

    part = width // X_SIZE
    turned = pl.pallas_call(
        functools.partial(turn_kernel, part // z_size),
        out_shape=jax.ShapeDtypeStruct((X_SIZE, part, tokens), BF16),
        in_specs=[whole()],
        out_specs=whole(),
        compiler_params=params(),
        name="turn",
    )(layer_input)
    layer_part = lax.all_to_all(turned, "x", split_axis=0, concat_axis=0, tiled=True)
    near = lax.all_gather(value_grad, "x", axis=0, tiled=False)
    all_value_grads = lax.all_gather(near, "t", axis=0, tiled=False)
    plane = pl.pallas_call(
        weight_kernel,
        out_shape=jax.ShapeDtypeStruct((part, all_value_grads.shape[0] * HD), BF16),
        in_specs=[whole()] * 2,
        out_specs=whole(),
        compiler_params=params(),
        name="weight",
    )(layer_part, all_value_grads)
    planes = lax.all_to_all(
        plane.reshape(z_size, part // z_size, -1), "z", split_axis=0, concat_axis=0, tiled=True
    )
    weight_grad = jnp.sum(planes.astype(F32), axis=0) * (1.0 / math.sqrt(tokens * dp_size))

    pairs = jnp.concatenate([key_rows, value_rows], axis=1)
    pairs, all_doc, all_place = lax.optimization_barrier((pairs, all_doc, all_place))
    all_pairs = lax.all_gather(pairs, DP, axis=0, tiled=True)
    same = run_doc[:, None] == all_doc.reshape(1, -1)
    at = jnp.arange(MAX_RUNS, dtype=jnp.int32)[:, None] == all_place.reshape(1, -1)
    ids = jnp.arange(dp_size * runs, dtype=jnp.int32)[None, :]
    place = exact_pick(same, jnp.where(at, ids // runs, 0)) * runs + exact_pick(same, jnp.where(at, ids % runs, 0))
    unroll = 4
    wide = (tokens, width)
    attended, query_grad = pl.pallas_call(
        functools.partial(home_kernel, group, unroll),
        out_shape=[jax.ShapeDtypeStruct(wide, BF16)] * 2,
        in_specs=[whole(pltpu.SMEM), whole(pltpu.SMEM), whole(), whole(), whole()],
        out_specs=[whole()] * 2,
        scratch_shapes=[
            pltpu.VMEM(all_pairs.shape, F32),
            pltpu.VMEM((unroll, MAX_RUNS * RUN, 2 * HD), F32),
            pltpu.VMEM(wide, F32), pltpu.VMEM(wide, F32), pltpu.VMEM(wide, F32), pltpu.VMEM(wide, F32),
        ],
        compiler_params=params(),
        name="home",
    )(place, run_place, query_rows, output_grad, all_pairs)
    return (attended, query_grad, key_grad, value_grad, weight_grad)


def solution(mesh):
    fine = Mesh(mesh.devices.reshape(-1, X_SIZE, mesh.shape["tensor"]), ("z", "x", "t"))
    rows = P(DP, "t")
    return jax.shard_map(
        shards,
        mesh=fine,
        in_specs=(rows, rows, rows, rows, rows, P(DP), P(DP), P()),
        out_specs=(rows, rows, rows, rows, P(("t",) + DP, None)),
        check_vma=False,
    )
```

```python
import functools
import math

import jax
import jax.numpy as jnp
from jax import lax
from jax.experimental import pallas as pl
from jax.experimental.pallas import tpu as pltpu
from jax.sharding import Mesh
from jax.sharding import PartitionSpec as P

HD = 128
RUN = 8
X_SIZE = 4
Z_LOW = 4
MAX_RUNS = 64
STEP_RUNS = 16
BRING = 4
TAG_ROWS = 16
NEG_FILL = -1e30
F32 = jnp.float32
BF16 = jnp.bfloat16
NT = (((1,), (1,)), ((), ()))
TN = (((0,), (0,)), ((), ()))
DP = ("zh", "zl", "x")


def whole(memory=pltpu.VMEM):
    return pl.BlockSpec(memory_space=memory)


def params(limit):
    return pltpu.CompilerParams(vmem_limit_bytes=limit * 1024 * 1024)


def slot_row(doc, servers):
    tokens, docs = doc.shape[1], servers.shape[1]
    same = lax.broadcasted_iota(jnp.int32, (docs, tokens), 0) == doc
    names = jnp.broadcast_to(servers.astype(F32), (RUN, docs)).astype(BF16)
    server = jnp.dot(names, same.astype(F32).astype(BF16), preferred_element_type=F32)[:1].astype(jnp.int32)
    return server * RUN + lax.broadcasted_iota(jnp.int32, (1, tokens), 1) % RUN


def one_hot(slots, slot):
    return (lax.broadcasted_iota(jnp.int32, (slots, slot.shape[1]), 0) == slot).astype(F32).astype(BF16)


def pack_kernel(
    doc_hbm, offset_hbm, servers_hbm, query_hbm, grad_hbm, key_hbm, value_hbm, out_hbm, pairs_ref, slot_ref,
    doc_ref, offset_ref, servers_ref, query_ref, grad_ref, key_ref, value_ref, out_ref, in_sems, out_sems,
):
    slots, tokens = out_ref.shape[0], doc_ref.shape[1]
    sources = (doc_hbm, offset_hbm, servers_hbm, query_hbm, grad_hbm, key_hbm, value_hbm)
    targets = (doc_ref, offset_ref, servers_ref, query_ref, grad_ref, key_ref, value_ref)
    arrivals = [pltpu.make_async_copy(a, b, in_sems.at[i]) for i, (a, b) in enumerate(zip(sources, targets))]
    for copy in arrivals:
        copy.start()
    for copy in arrivals[:3]:
        copy.wait()
    doc = doc_ref[...]
    slot = slot_row(doc, servers_ref[...])
    slot_ref[...] = jnp.broadcast_to(slot, slot_ref.shape)
    hot = one_hot(slots, slot)
    place = offset_ref[...] // RUN
    line = lax.broadcasted_iota(jnp.int32, (HD, tokens), 0)
    tags = jnp.where(line == 0, doc + 1, jnp.where(line == 1, place, 0)).astype(F32).astype(BF16)
    tags = lax.dot_general(hot, tags, NT, preferred_element_type=F32).astype(BF16)
    departures = []

    def send(begin, end):
        columns = pl.ds(begin, end - begin)
        copy = pltpu.make_async_copy(out_ref.at[:, columns], out_hbm.at[:, columns], out_sems.at[len(departures)])
        copy.start()
        departures.append(copy)

    at = 0
    for copy, ref in zip(arrivals[3:], targets[3:]):
        copy.wait()
        width = ref.shape[1]
        out_ref[:, at : at + width] = jnp.dot(hot, ref[...], preferred_element_type=F32).astype(BF16)
        at += width
        if width > HD:
            send(at - width, at)
    out_ref[:, at : at + HD] = tags
    send(at - 2 * HD, at + HD)
    pairs_ref[:tokens, :HD] = key_ref[...]
    pairs_ref[:tokens, HD:] = value_ref[...]
    line = lax.broadcasted_iota(jnp.int32, (TAG_ROWS, tokens), 0)
    tags = jnp.where(line == 0, doc, jnp.where(line == 1, place, 0)).astype(F32).astype(BF16)
    pairs_ref[tokens:, :] = jnp.zeros((TAG_ROWS, 2 * HD), BF16)
    pairs_ref[tokens:, :tokens] = tags
    for copy in departures:
        copy.wait()


def turn_kernel(z_high, z_low, me_ref, layer_hbm, *refs):
    outs, layer_ref, sem = refs[:X_SIZE], refs[X_SIZE], refs[X_SIZE + 1]
    copy = pltpu.make_async_copy(layer_hbm, layer_ref, sem)
    copy.start()
    width = layer_ref.shape[1]
    rows = width // X_SIZE
    deep = rows // (z_high * z_low)
    new = lax.broadcasted_iota(jnp.int32, (rows, width), 0)
    old = lax.broadcasted_iota(jnp.int32, (rows, width), 1)
    ahead = old - (new // deep * (X_SIZE * deep) + new % deep)
    copy.wait()
    for d in range(X_SIZE):
        hot = (ahead == (me_ref[0] + d) % X_SIZE * deep).astype(F32).astype(BF16)
        outs[d][...] = lax.dot_general(hot, layer_ref[...], NT, preferred_element_type=F32).astype(BF16)


def server_kernel(group, tag_ref, query_ref, grad_ref, key_ref, value_ref, out_ref, bias, key_acc, value_acc):
    head = pl.program_id(0)

    @pl.when(head == 0)
    def _():
        slots = tag_ref.shape[0]
        tags = tag_ref[...].astype(F32)
        turned = tags.T
        col_doc, row_doc = tags[:, 0:1], turned[0:1, :]
        col_pos = tags[:, 1:2] * RUN + (lax.broadcasted_iota(jnp.int32, (slots, 1), 0) % RUN).astype(F32)
        row_pos = turned[1:2, :] * RUN + (lax.broadcasted_iota(jnp.int32, (1, slots), 1) % RUN).astype(F32)
        bias[...] = jnp.where((col_doc == row_doc) & (col_pos <= row_pos), 0.0, NEG_FILL)
        key_acc[...] = jnp.zeros_like(key_acc)
        value_acc[...] = jnp.zeros_like(value_acc)

    scale = float(HD) ** (-0.5)
    query, grad = query_ref[...], grad_ref[...]
    scores = lax.dot_general(key_ref[...], query, NT, preferred_element_type=F32) + bias[...]
    top = jnp.max(scores, axis=0, keepdims=True)
    exp_scores = jnp.exp((scores - top) * scale)
    total = jnp.sum(exp_scores, axis=0, keepdims=True)
    weights = exp_scores * (1.0 / total)
    weights_low = weights.astype(BF16)
    grad_weights = lax.dot_general(value_ref[...], grad, NT, preferred_element_type=F32)
    row_delta = jnp.sum(weights_low.astype(F32) * grad_weights, axis=0, keepdims=True)
    grad_scores = (weights * (grad_weights - row_delta)).astype(BF16)
    value_acc[...] += jnp.dot(weights_low, grad, preferred_element_type=F32)
    key_acc[...] += jnp.dot(grad_scores, query, preferred_element_type=F32)

    @pl.when(head == group - 1)
    def _():
        out_ref[:, :HD] = (key_acc[...] * scale).astype(BF16)
        out_ref[:, HD:] = value_acc[...].astype(BF16)


def home_kernel(
    group, unroll, place_ref, reach_ref, query_hbm, grad_hbm, pairs_ref, mixed_ref, query_grad_ref,
    rows, query_ref, grad_ref, query, grad, mixed, query_grad, sems,
):
    scale = float(HD) ** (-0.5)
    count = query_ref.shape[0] // RUN
    arrivals = [
        pltpu.make_async_copy(query_hbm, query_ref, sems.at[0]),
        pltpu.make_async_copy(grad_hbm, grad_ref, sems.at[1]),
    ]
    for copy in arrivals:
        copy.start()
    rows[...] = jnp.zeros_like(rows)
    for copy in arrivals:
        copy.wait()
    query[...] = query_ref[...].astype(F32)
    grad[...] = grad_ref[...].astype(F32)

    def stack(ref, run):
        parts = [ref[pl.ds(pl.multiple_of(run * RUN, RUN), RUN), h * HD : (h + 1) * HD] for h in range(group)]
        return jnp.concatenate(parts, axis=0)

    def unstack(ref, run, block):
        for h in range(group):
            ref[pl.ds(pl.multiple_of(run * RUN, RUN), RUN), h * HD : (h + 1) * HD] = block[h * RUN : (h + 1) * RUN]

    def bring(u, run):
        def several(i, carry):
            for j in range(BRING):
                k = i * BRING + j
                place = place_ref[run, k]
                two = pairs_ref[pl.ds(pl.multiple_of(place // 2 * (2 * RUN), 2 * RUN), 2 * RUN), :].astype(F32)
                one = jnp.where(place % 2 == 1, two[RUN:], two[:RUN])
                rows[u, pl.ds(pl.multiple_of(k * RUN, RUN), RUN), :] = one
            return carry

        lax.fori_loop(0, reach_ref[run] // BRING + 1, several, 0)

    def part(index, reach_runs):
        reach_rows = reach_runs * RUN
        for u in range(unroll):
            bring(u, index * unroll + u)
        rows_each = group * RUN
        token = lax.broadcasted_iota(jnp.int32, (rows_each, reach_rows), 0) % RUN
        ahead = lax.broadcasted_iota(jnp.int32, (rows_each, reach_rows), 1) - token
        each = range(unroll)
        cut = lambda block: [block[u * rows_each : (u + 1) * rows_each] for u in each]
        runs = [index * unroll + u for u in each]
        blocks = [rows[u, :reach_rows].astype(BF16) for u in each]
        keys, values = [block[:, :HD] for block in blocks], [block[:, HD:] for block in blocks]
        query_runs = [stack(query, run).astype(BF16) for run in runs]
        grad_full = jnp.concatenate([stack(grad, run) for run in runs], axis=0)
        grad_runs = cut(grad_full.astype(BF16))
        dots = lambda left, right: [lax.dot_general(left[u], right[u], NT, preferred_element_type=F32) for u in each]
        scores = dots(query_runs, keys)
        scores = [jnp.where(ahead <= reach_ref[runs[u]] * RUN, scores[u], NEG_FILL) for u in each]
        scores = jnp.concatenate(scores, axis=0)
        grad_weights = jnp.concatenate(dots(grad_runs, values), axis=0)
        top = jnp.max(scores, axis=1, keepdims=True)
        exp_scores = jnp.exp((scores - top) * scale)
        total = jnp.sum(exp_scores, axis=1, keepdims=True)
        weights = exp_scores * (1.0 / total)
        low = cut(weights.astype(BF16))
        mixed_full = [jnp.dot(low[u], values[u], preferred_element_type=F32) for u in each]
        row_delta = jnp.sum(grad_full * jnp.concatenate(mixed_full, axis=0), axis=1, keepdims=True)
        grad_scores = cut((weights * (grad_weights - row_delta)).astype(BF16))
        back = [jnp.dot(grad_scores[u], keys[u], preferred_element_type=F32) * scale for u in each]
        for u in each:
            unstack(mixed, runs[u], mixed_full[u])
            unstack(query_grad, runs[u], back[u])

    def step(index, carry):
        reach = reach_ref[index * unroll]
        for u in range(1, unroll):
            reach = jnp.maximum(reach, reach_ref[index * unroll + u])
        below = 0
        for reach_runs in (STEP_RUNS, 2 * STEP_RUNS, MAX_RUNS):
            pl.when((reach >= below) & (reach < reach_runs))(functools.partial(part, index, reach_runs))
            below = reach_runs
        return carry

    lax.fori_loop(0, count // unroll, step, 0)
    mixed_ref[...] = mixed[...].astype(BF16)
    query_grad_ref[...] = query_grad[...].astype(BF16)


def own_kernel(slot_ref, back_ref, key_grad_ref, value_grad_ref, near_ref):
    hot = one_hot(back_ref.shape[0], slot_ref[:1])
    rows = lax.dot_general(hot, back_ref[...], TN, preferred_element_type=F32).astype(BF16)
    key_grad_ref[...] = rows[:, :HD]
    value_grad_ref[...] = rows[:, HD:]
    for i in range(near_ref.shape[0]):
        near_ref[i] = rows[:, HD:]


def weight_kernel(x_ref, core_ref, *refs):
    layers, own_ref, other_ref, out_ref = refs[:X_SIZE], refs[X_SIZE], refs[X_SIZE + 1], refs[X_SIZE + 2]
    me, core = x_ref[0], core_ref[0]
    y_size = own_ref.shape[0] // X_SIZE
    for y in range(y_size):
        for grads, c in ((own_ref, core), (other_ref, 1 - core)):
            total = jnp.dot(layers[0][...], grads[me * y_size + y], preferred_element_type=F32)
            for d in range(1, X_SIZE):
                there = (me - d + X_SIZE) % X_SIZE
                total += jnp.dot(layers[d][...], grads[there * y_size + y], preferred_element_type=F32)
            out_ref[:, pl.ds(pl.multiple_of((2 * y + c) * HD, HD), HD)] = total.astype(BF16)


def exact_pick(left, right):
    return lax.dot_general(left.astype(BF16), right.astype(BF16), NT, preferred_element_type=F32).astype(jnp.int32)


def shards(query_rows, key_rows, value_rows, output_grad, layer_input, token_document, token_offset, document_server):
    dp_size = lax.axis_size(DP)
    high, low = lax.axis_size("zh"), lax.axis_size("zl")
    tokens = query_rows.shape[0]
    runs = tokens // RUN
    slots = dp_size * RUN
    width = query_rows.shape[1]
    group = width // HD
    doc, offset, servers = token_document[None, :], token_offset[None, :], document_server[None, :]
    x_index, core = lax.axis_index("x").astype(jnp.int32), lax.axis_index("c").astype(jnp.int32)
    x_index, core = x_index.reshape(1), core.reshape(1)

    def call(kernel, out_shape, *args, **more):
        shapes = [jax.ShapeDtypeStruct(shape, BF16) if isinstance(shape, tuple) else shape for shape in out_shape]
        out = pl.pallas_call(
            kernel,
            out_shape=shapes,
            in_specs=more.pop("in_specs", [whole()] * len(args)),
            out_specs=more.pop("out_specs", [whole()] * len(shapes)),
            compiler_params=params(more.pop("limit", 32)),
            **more,
        )(*args)
        return out[0] if len(shapes) == 1 else list(out)

    def swap(block, axis):
        return lax.all_to_all(block, axis, split_axis=0, concat_axis=0, tiled=True)

    sent, pairs, slot = call(
        pack_kernel,
        [(slots, 2 * width + 3 * HD), (tokens + TAG_ROWS, 2 * HD), jax.ShapeDtypeStruct((RUN, tokens), jnp.int32)],
        doc, offset, servers, query_rows, output_grad, key_rows, value_rows,
        in_specs=[whole(pltpu.HBM)] * 7,
        out_specs=[whole(pltpu.HBM), whole(), whole()],
        scratch_shapes=[pltpu.VMEM((1, tokens), jnp.int32)] * 2 + [pltpu.VMEM(servers.shape, jnp.int32)]
        + [pltpu.VMEM((tokens, width), BF16)] * 2 + [pltpu.VMEM((tokens, HD), BF16)] * 2
        + [pltpu.VMEM((slots, 2 * width + 3 * HD), BF16), pltpu.SemaphoreType.DMA((7,)), pltpu.SemaphoreType.DMA((3,))],
        limit=60,
        name="pack",
    )
    part = width // X_SIZE
    sent, layer_input, pairs = lax.optimization_barrier((sent, layer_input, pairs))
    arrived = swap(sent.reshape(dp_size, RUN, -1), DP)
    turned = call(
        functools.partial(turn_kernel, high, low), [(part, tokens)] * X_SIZE, x_index, layer_input,
        in_specs=[whole(pltpu.SMEM), whole(pltpu.HBM)],
        scratch_shapes=[pltpu.VMEM((tokens, width), BF16), pltpu.SemaphoreType.DMA],
        limit=60,
        name="turn",
    )
    turned[0], pairs = lax.optimization_barrier((turned[0], pairs))
    all_pairs = lax.all_gather(pairs, DP, axis=0, tiled=True)
    layers = [turned[0]] + [
        lax.ppermute(turned[d], "x", [(i, (i + d) % X_SIZE) for i in range(X_SIZE)]) for d in range(1, X_SIZE)
    ]
    arrived, *layers = lax.optimization_barrier((arrived, *layers))
    arrived = arrived.reshape(slots, -1)

    column = lambda at: pl.BlockSpec((slots, HD), lambda h, at=at: (0, at + h))
    fixed = lambda at: pl.BlockSpec((slots, HD), lambda h, at=at: (0, at))
    served = call(
        functools.partial(server_kernel, group), [(slots, 2 * HD)], *[arrived] * 5,
        grid=(group,),
        in_specs=[fixed(2 * group + 2), column(0), column(group), fixed(2 * group), fixed(2 * group + 1)],
        out_specs=[pl.BlockSpec((slots, 2 * HD), lambda h: (0, 0))],
        scratch_shapes=[pltpu.VMEM((slots, slots), F32), pltpu.VMEM((slots, HD), F32), pltpu.VMEM((slots, HD), F32)],
        name="server",
    )

    back = swap(served.reshape(dp_size, RUN, -1), DP).reshape(slots, -1)
    key_grad, value_grad, near = call(
        own_kernel, [(tokens, HD), (tokens, HD), (X_SIZE * lax.axis_size("y"), tokens, HD)], slot, back, name="own"
    )

    y_size = lax.axis_size("y")
    own_core = swap(near, ("x", "y"))
    other_core = lax.ppermute(own_core, "c", [(0, 1), (1, 0)])
    channels = 2 * y_size * HD
    plane = call(
        weight_kernel, [(part, channels)], x_index, core, *layers, own_core, other_core,
        in_specs=[whole(pltpu.SMEM)] * 2 + [whole()] * (X_SIZE + 2), name="weight",
    )
    plane, all_pairs = lax.optimization_barrier((plane, all_pairs))
    block = swap(plane.reshape(high * low, part // (high * low), channels), ("zh", "zl"))
    weight_grad = jnp.sum(block.astype(F32), axis=0) * (1.0 / math.sqrt(tokens * dp_size))

    tags = all_pairs.reshape(dp_size, tokens + TAG_ROWS, 2 * HD)[:, tokens : tokens + 2, :tokens:RUN]
    all_doc, all_place = tags[:, 0].reshape(1, -1), tags[:, 1].reshape(1, -1)
    run_doc, run_place = token_document[::RUN], token_offset[::RUN] // RUN
    same = run_doc.astype(BF16)[:, None] == all_doc
    at = jnp.arange(MAX_RUNS, dtype=jnp.int32).astype(BF16)[:, None] == all_place
    ids = jnp.arange(dp_size * runs, dtype=jnp.int32)[None, :]
    device, run = exact_pick(same, jnp.where(at, ids // runs, 0)), exact_pick(same, jnp.where(at, ids % runs, 0))
    place = device * (runs + TAG_ROWS // RUN) + run
    unroll = 8
    wide = (tokens, width)
    attended, query_grad = call(
        functools.partial(home_kernel, group, unroll), [wide, wide],
        place, run_place, query_rows, output_grad, all_pairs,
        in_specs=[whole(pltpu.SMEM), whole(pltpu.SMEM), whole(pltpu.HBM), whole(pltpu.HBM), whole()],
        scratch_shapes=[pltpu.VMEM((unroll, MAX_RUNS * RUN, 2 * HD), F32)] + [pltpu.VMEM(wide, BF16)] * 2
        + [pltpu.VMEM(wide, F32)] * 4 + [pltpu.SemaphoreType.DMA((2,))],
        limit=60,
        name="home",
    )
    return (attended, query_grad, key_grad, value_grad, weight_grad)


def solution(mesh):
    shape = (-1, Z_LOW, X_SIZE, mesh.shape["tensor"] // 2, 2)
    fine = Mesh(mesh.devices.reshape(shape), ("zh", "zl", "x", "y", "c"))
    rows = P(DP, ("y", "c"))
    return jax.shard_map(
        shards,
        mesh=fine,
        in_specs=(rows, rows, rows, rows, rows, P(DP), P(DP), P()),
        out_specs=(rows, rows, rows, rows, P(("y", "c") + DP, None)),
        check_vma=False,
    )
```

```python
import functools
import math

import jax
import jax.numpy as jnp
from jax import lax
from jax.experimental import pallas as pl
from jax.experimental.pallas import tpu as pltpu
from jax.sharding import Mesh
from jax.sharding import PartitionSpec as P

HD = 128
RUN = 8
X_SIZE = 4
Z_LOW = 4
MAX_RUNS = 64
STEP_RUNS = 16
BRING = 4
LOG2_E = math.log2(math.e)
SERVER_HEADS = 4
TAG_ROWS = 16
NEG_FILL = -1e30
F32 = jnp.float32
BF16 = jnp.bfloat16
NT = (((1,), (1,)), ((), ()))
TN = (((0,), (0,)), ((), ()))
DP = ("zh", "zl", "x")


def whole(memory=pltpu.VMEM):
    return pl.BlockSpec(memory_space=memory)


def params(limit):
    return pltpu.CompilerParams(vmem_limit_bytes=limit * 1024 * 1024)


def slot_row(doc, servers):
    tokens, docs = doc.shape[1], servers.shape[1]
    same = lax.broadcasted_iota(jnp.int32, (docs, tokens), 0) == doc
    names = jnp.broadcast_to(servers.astype(F32), (RUN, docs)).astype(BF16)
    server = jnp.dot(names, same.astype(F32).astype(BF16), preferred_element_type=F32)[:1].astype(jnp.int32)
    return server * RUN + lax.broadcasted_iota(jnp.int32, (1, tokens), 1) % RUN


def one_hot(slots, slot):
    return (lax.broadcasted_iota(jnp.int32, (slots, slot.shape[1]), 0) == slot).astype(F32).astype(BF16)


def pack_kernel(
    doc_hbm, offset_hbm, servers_hbm, query_hbm, grad_hbm, key_hbm, value_hbm, out_hbm, pairs_ref, slot_ref,
    doc_ref, offset_ref, servers_ref, query_ref, grad_ref, key_ref, value_ref, out_ref, in_sems, out_sems,
):
    slots, tokens = out_ref.shape[0], doc_ref.shape[1]
    sources = (doc_hbm, offset_hbm, servers_hbm, query_hbm, grad_hbm, key_hbm, value_hbm)
    targets = (doc_ref, offset_ref, servers_ref, query_ref, grad_ref, key_ref, value_ref)
    arrivals = [pltpu.make_async_copy(a, b, in_sems.at[i]) for i, (a, b) in enumerate(zip(sources, targets))]
    for copy in arrivals:
        copy.start()
    for copy in arrivals[:3]:
        copy.wait()
    doc = doc_ref[...]
    slot = slot_row(doc, servers_ref[...])
    slot_ref[...] = jnp.broadcast_to(slot, slot_ref.shape)
    hot = one_hot(slots, slot)
    place = offset_ref[...] // RUN
    line = lax.broadcasted_iota(jnp.int32, (HD, tokens), 0)
    tags = jnp.where(line == 0, doc + 1, jnp.where(line == 1, place, 0)).astype(F32).astype(BF16)
    tags = lax.dot_general(hot, tags, NT, preferred_element_type=F32).astype(BF16)
    departures = []

    def send(begin, end):
        columns = pl.ds(begin, end - begin)
        copy = pltpu.make_async_copy(out_ref.at[:, columns], out_hbm.at[:, columns], out_sems.at[len(departures)])
        copy.start()
        departures.append(copy)

    at = 0
    for copy, ref in zip(arrivals[3:], targets[3:]):
        copy.wait()
        width = ref.shape[1]
        out_ref[:, at : at + width] = jnp.dot(hot, ref[...], preferred_element_type=F32).astype(BF16)
        at += width
        if width > HD:
            send(at - width, at)
    out_ref[:, at : at + HD] = tags
    send(at - 2 * HD, at + HD)
    pairs_ref[:tokens, :HD] = key_ref[...]
    pairs_ref[:tokens, HD:] = value_ref[...]
    line = lax.broadcasted_iota(jnp.int32, (TAG_ROWS, tokens), 0)
    tags = jnp.where(line == 0, doc, jnp.where(line == 1, place, 0)).astype(F32).astype(BF16)
    pairs_ref[tokens:, :] = jnp.zeros((TAG_ROWS, 2 * HD), BF16)
    pairs_ref[tokens:, :tokens] = tags
    for copy in departures:
        copy.wait()


def turn_kernel(z_high, z_low, me_ref, layer_hbm, *refs):
    outs, layer_ref, sem = refs[:X_SIZE], refs[X_SIZE], refs[X_SIZE + 1]
    copy = pltpu.make_async_copy(layer_hbm, layer_ref, sem)
    copy.start()
    width = layer_ref.shape[1]
    rows = width // X_SIZE
    deep = rows // (z_high * z_low)
    new = lax.broadcasted_iota(jnp.int32, (rows, width), 0)
    old = lax.broadcasted_iota(jnp.int32, (rows, width), 1)
    ahead = old - (new // deep * (X_SIZE * deep) + new % deep)
    copy.wait()
    for d in range(X_SIZE):
        hot = (ahead == (me_ref[0] + d) % X_SIZE * deep).astype(F32).astype(BF16)
        outs[d][...] = lax.dot_general(hot, layer_ref[...], NT, preferred_element_type=F32).astype(BF16)


def server_kernel(tag_ref, query_ref, grad_ref, key_ref, value_ref, out_ref, bias, key_acc, value_acc):
    head = pl.program_id(0)

    @pl.when(head == 0)
    def _():
        slots = tag_ref.shape[0]
        tags = tag_ref[...].astype(F32)
        turned = tags.T
        col_doc, row_doc = tags[:, 0:1], turned[0:1, :]
        col_pos = tags[:, 1:2] * RUN + (lax.broadcasted_iota(jnp.int32, (slots, 1), 0) % RUN).astype(F32)
        row_pos = turned[1:2, :] * RUN + (lax.broadcasted_iota(jnp.int32, (1, slots), 1) % RUN).astype(F32)
        bias[...] = jnp.where((col_doc == row_doc) & (col_pos <= row_pos), 0.0, NEG_FILL)
        key_acc[...] = jnp.zeros_like(key_acc)
        value_acc[...] = jnp.zeros_like(value_acc)

    scale = float(HD) ** (-0.5)
    key, value = key_ref[...], value_ref[...]
    heads = range(query_ref.shape[1] // HD)
    cut = lambda ref: [ref[:, h * HD : (h + 1) * HD] for h in heads]
    query, grad = cut(query_ref), cut(grad_ref)
    scores = [lax.dot_general(key, query[h], NT, preferred_element_type=F32) + bias[...] for h in heads]
    grad_weights = [lax.dot_general(value, grad[h], NT, preferred_element_type=F32) for h in heads]
    key_part, value_part = key_acc[...], value_acc[...]
    for h in heads:
        top = jnp.max(scores[h], axis=0, keepdims=True)
        exp_scores = jnp.exp2((scores[h] - top) * (scale * LOG2_E))
        total = jnp.sum(exp_scores, axis=0, keepdims=True)
        weights = exp_scores * (1.0 / total)
        weights_low = weights.astype(BF16)
        row_delta = jnp.sum(weights_low.astype(F32) * grad_weights[h], axis=0, keepdims=True)
        grad_scores = (weights * (grad_weights[h] - row_delta)).astype(BF16)
        value_part += jnp.dot(weights_low, grad[h], preferred_element_type=F32)
        key_part += jnp.dot(grad_scores, query[h], preferred_element_type=F32)
    key_acc[...] = key_part
    value_acc[...] = value_part

    @pl.when(head == pl.num_programs(0) - 1)
    def _():
        out_ref[:, :HD] = (key_acc[...] * scale).astype(BF16)
        out_ref[:, HD:] = value_acc[...].astype(BF16)


def home_kernel(
    group, unroll, place_ref, reach_ref, query_hbm, grad_hbm, pairs_ref, mixed_ref, query_grad_ref,
    rows, query_ref, grad_ref, query, grad, mixed, query_grad, sems,
):
    scale = float(HD) ** (-0.5)
    count = query_ref.shape[0] // RUN
    arrivals = [
        pltpu.make_async_copy(query_hbm, query_ref, sems.at[0]),
        pltpu.make_async_copy(grad_hbm, grad_ref, sems.at[1]),
    ]
    for copy in arrivals:
        copy.start()
    rows[...] = jnp.zeros_like(rows)
    for copy in arrivals:
        copy.wait()
    query[...] = query_ref[...].astype(F32)
    grad[...] = grad_ref[...].astype(F32)

    def stack(ref, run):
        parts = [ref[pl.ds(pl.multiple_of(run * RUN, RUN), RUN), h * HD : (h + 1) * HD] for h in range(group)]
        return jnp.concatenate(parts, axis=0)

    def unstack(ref, run, block):
        for h in range(group):
            ref[pl.ds(pl.multiple_of(run * RUN, RUN), RUN), h * HD : (h + 1) * HD] = block[h * RUN : (h + 1) * RUN]

    def bring(u, run):
        def several(i, carry):
            for j in range(BRING):
                k = i * BRING + j
                place = place_ref[run, k]
                two = pairs_ref[pl.ds(pl.multiple_of(place // 2 * (2 * RUN), 2 * RUN), 2 * RUN), :].astype(F32)
                one = jnp.where(place % 2 == 1, two[RUN:], two[:RUN])
                rows[u, pl.ds(pl.multiple_of(k * RUN, RUN), RUN), :] = one
            return carry

        lax.fori_loop(0, reach_ref[run] // BRING + 1, several, 0)

    def part(index, reach_runs):
        reach_rows = reach_runs * RUN
        for u in range(unroll):
            bring(u, index * unroll + u)
        rows_each = group * RUN
        token = lax.broadcasted_iota(jnp.int32, (rows_each, reach_rows), 0) % RUN
        ahead = lax.broadcasted_iota(jnp.int32, (rows_each, reach_rows), 1) - token
        each = range(unroll)
        cut = lambda block: [block[u * rows_each : (u + 1) * rows_each] for u in each]
        runs = [index * unroll + u for u in each]
        blocks = [rows[u, :reach_rows].astype(BF16) for u in each]
        keys, values = [block[:, :HD] for block in blocks], [block[:, HD:] for block in blocks]
        query_runs = [stack(query, run).astype(BF16) for run in runs]
        grad_full = jnp.concatenate([stack(grad, run) for run in runs], axis=0)
        grad_runs = cut(grad_full.astype(BF16))
        dots = lambda left, right: [lax.dot_general(left[u], right[u], NT, preferred_element_type=F32) for u in each]
        scores = dots(query_runs, keys)
        scores = [jnp.where(ahead <= reach_ref[runs[u]] * RUN, scores[u], NEG_FILL) for u in each]
        scores = jnp.concatenate(scores, axis=0)
        grad_weights = jnp.concatenate(dots(grad_runs, values), axis=0)
        top = jnp.max(scores, axis=1, keepdims=True)
        exp_scores = jnp.exp((scores - top) * scale)
        total = jnp.sum(exp_scores, axis=1, keepdims=True)
        weights = exp_scores * (1.0 / total)
        low = cut(weights.astype(BF16))
        mixed_full = [jnp.dot(low[u], values[u], preferred_element_type=F32) for u in each]
        row_delta = jnp.sum(grad_full * jnp.concatenate(mixed_full, axis=0), axis=1, keepdims=True)
        grad_scores = cut((weights * (grad_weights - row_delta)).astype(BF16))
        back = [jnp.dot(grad_scores[u], keys[u], preferred_element_type=F32) * scale for u in each]
        for u in each:
            unstack(mixed, runs[u], mixed_full[u])
            unstack(query_grad, runs[u], back[u])

    def step(index, carry):
        reach = reach_ref[index * unroll]
        for u in range(1, unroll):
            reach = jnp.maximum(reach, reach_ref[index * unroll + u])
        below = 0
        for reach_runs in (STEP_RUNS, 2 * STEP_RUNS, MAX_RUNS):
            pl.when((reach >= below) & (reach < reach_runs))(functools.partial(part, index, reach_runs))
            below = reach_runs
        return carry

    lax.fori_loop(0, count // unroll, step, 0)
    mixed_ref[...] = mixed[...].astype(BF16)
    query_grad_ref[...] = query_grad[...].astype(BF16)


def own_kernel(slot_ref, back_ref, key_grad_ref, value_grad_ref, near_ref):
    hot = one_hot(back_ref.shape[0], slot_ref[:1])
    rows = lax.dot_general(hot, back_ref[...], TN, preferred_element_type=F32).astype(BF16)
    key_grad_ref[...] = rows[:, :HD]
    value_grad_ref[...] = rows[:, HD:]
    for i in range(near_ref.shape[0]):
        near_ref[i] = rows[:, HD:]


def weight_kernel(x_ref, core_ref, *refs):
    layers, own_ref, other_ref, out_ref = refs[:X_SIZE], refs[X_SIZE], refs[X_SIZE + 1], refs[X_SIZE + 2]
    me, core = x_ref[0], core_ref[0]
    y_size = own_ref.shape[0] // X_SIZE
    for y in range(y_size):
        for grads, c in ((own_ref, core), (other_ref, 1 - core)):
            total = jnp.dot(layers[0][...], grads[me * y_size + y], preferred_element_type=F32)
            for d in range(1, X_SIZE):
                there = (me - d + X_SIZE) % X_SIZE
                total += jnp.dot(layers[d][...], grads[there * y_size + y], preferred_element_type=F32)
            out_ref[:, pl.ds(pl.multiple_of((2 * y + c) * HD, HD), HD)] = total.astype(BF16)


def exact_pick(left, right):
    return lax.dot_general(left.astype(BF16), right.astype(BF16), NT, preferred_element_type=F32).astype(jnp.int32)


def shards(query_rows, key_rows, value_rows, output_grad, layer_input, token_document, token_offset, document_server):
    dp_size = lax.axis_size(DP)
    high, low = lax.axis_size("zh"), lax.axis_size("zl")
    tokens = query_rows.shape[0]
    runs = tokens // RUN
    slots = dp_size * RUN
    width = query_rows.shape[1]
    group = width // HD
    doc, offset, servers = token_document[None, :], token_offset[None, :], document_server[None, :]
    x_index, core = lax.axis_index("x").astype(jnp.int32), lax.axis_index("c").astype(jnp.int32)
    x_index, core = x_index.reshape(1), core.reshape(1)

    def call(kernel, out_shape, *args, **more):
        shapes = [jax.ShapeDtypeStruct(shape, BF16) if isinstance(shape, tuple) else shape for shape in out_shape]
        out = pl.pallas_call(
            kernel,
            out_shape=shapes,
            in_specs=more.pop("in_specs", [whole()] * len(args)),
            out_specs=more.pop("out_specs", [whole()] * len(shapes)),
            compiler_params=params(more.pop("limit", 32)),
            **more,
        )(*args)
        return out[0] if len(shapes) == 1 else list(out)

    def swap(block, axis):
        return lax.all_to_all(block, axis, split_axis=0, concat_axis=0, tiled=True)

    sent, pairs, slot = call(
        pack_kernel,
        [(slots, 2 * width + 3 * HD), (tokens + TAG_ROWS, 2 * HD), jax.ShapeDtypeStruct((RUN, tokens), jnp.int32)],
        doc, offset, servers, query_rows, output_grad, key_rows, value_rows,
        in_specs=[whole(pltpu.HBM)] * 7,
        out_specs=[whole(pltpu.HBM), whole(), whole()],
        scratch_shapes=[pltpu.VMEM((1, tokens), jnp.int32)] * 2 + [pltpu.VMEM(servers.shape, jnp.int32)]
        + [pltpu.VMEM((tokens, width), BF16)] * 2 + [pltpu.VMEM((tokens, HD), BF16)] * 2
        + [pltpu.VMEM((slots, 2 * width + 3 * HD), BF16), pltpu.SemaphoreType.DMA((7,)), pltpu.SemaphoreType.DMA((3,))],
        limit=60,
        name="pack",
    )
    part = width // X_SIZE
    sent, layer_input, pairs = lax.optimization_barrier((sent, layer_input, pairs))
    arrived = swap(sent.reshape(dp_size, RUN, -1), DP)
    turned = call(
        functools.partial(turn_kernel, high, low), [(part, tokens)] * X_SIZE, x_index, layer_input,
        in_specs=[whole(pltpu.SMEM), whole(pltpu.HBM)],
        scratch_shapes=[pltpu.VMEM((tokens, width), BF16), pltpu.SemaphoreType.DMA],
        limit=60,
        name="turn",
    )
    all_pairs = lax.all_gather(pairs, DP, axis=0, tiled=True)
    layers = [turned[0]] + [
        lax.ppermute(turned[d], "x", [(i, (i + d) % X_SIZE) for i in range(X_SIZE)]) for d in range(1, X_SIZE)
    ]
    arrived, *layers = lax.optimization_barrier((arrived, *layers))
    arrived = arrived.reshape(slots, -1)

    steps = group // SERVER_HEADS
    column = lambda at: pl.BlockSpec((slots, SERVER_HEADS * HD), lambda h, at=at: (0, at + h))
    fixed = lambda at: pl.BlockSpec((slots, HD), lambda h, at=at: (0, at))
    served = call(
        server_kernel, [(slots, 2 * HD)], *[arrived] * 5,
        grid=(steps,),
        in_specs=[fixed(2 * group + 2), column(0), column(steps), fixed(2 * group), fixed(2 * group + 1)],
        out_specs=[pl.BlockSpec((slots, 2 * HD), lambda h: (0, 0))],
        scratch_shapes=[pltpu.VMEM((slots, slots), F32), pltpu.VMEM((slots, HD), F32), pltpu.VMEM((slots, HD), F32)],
        name="server",
    )

    back = swap(served.reshape(dp_size, RUN, -1), DP).reshape(slots, -1)
    key_grad, value_grad, near = call(
        own_kernel, [(tokens, HD), (tokens, HD), (X_SIZE * lax.axis_size("y"), tokens, HD)], slot, back, name="own"
    )

    y_size = lax.axis_size("y")
    own_core = swap(near, ("x", "y"))
    other_core = lax.ppermute(own_core, "c", [(0, 1), (1, 0)])
    channels = 2 * y_size * HD
    plane = call(
        weight_kernel, [(part, channels)], x_index, core, *layers, own_core, other_core,
        in_specs=[whole(pltpu.SMEM)] * 2 + [whole()] * (X_SIZE + 2), name="weight",
    )
    plane, all_pairs = lax.optimization_barrier((plane, all_pairs))
    block = swap(plane.reshape(high * low, part // (high * low), channels), ("zh", "zl"))
    weight_grad = jnp.sum(block.astype(F32), axis=0) * (1.0 / math.sqrt(tokens * dp_size))

    tags = all_pairs.reshape(dp_size, tokens + TAG_ROWS, 2 * HD)[:, tokens : tokens + 2, :tokens:RUN]
    all_doc, all_place = tags[:, 0].reshape(1, -1), tags[:, 1].reshape(1, -1)
    run_doc, run_place = token_document[::RUN], token_offset[::RUN] // RUN
    same = run_doc.astype(BF16)[:, None] == all_doc
    at = jnp.arange(MAX_RUNS, dtype=jnp.int32).astype(BF16)[:, None] == all_place
    ids = jnp.arange(dp_size * runs, dtype=jnp.int32)[None, :]
    device, run = exact_pick(same, jnp.where(at, ids // runs, 0)), exact_pick(same, jnp.where(at, ids % runs, 0))
    place = device * (runs + TAG_ROWS // RUN) + run
    unroll = 8
    wide = (tokens, width)
    attended, query_grad = call(
        functools.partial(home_kernel, group, unroll), [wide, wide],
        place, run_place, query_rows, output_grad, all_pairs,
        in_specs=[whole(pltpu.SMEM), whole(pltpu.SMEM), whole(pltpu.HBM), whole(pltpu.HBM), whole()],
        scratch_shapes=[pltpu.VMEM((unroll, MAX_RUNS * RUN, 2 * HD), F32)] + [pltpu.VMEM(wide, BF16)] * 2
        + [pltpu.VMEM(wide, F32)] * 4 + [pltpu.SemaphoreType.DMA((2,))],
        limit=60,
        name="home",
    )
    return (attended, query_grad, key_grad, value_grad, weight_grad)


def solution(mesh):
    shape = (-1, Z_LOW, X_SIZE, mesh.shape["tensor"] // 2, 2)
    fine = Mesh(mesh.devices.reshape(shape), ("zh", "zl", "x", "y", "c"))
    rows = P(DP, ("y", "c"))
    return jax.shard_map(
        shards,
        mesh=fine,
        in_specs=(rows, rows, rows, rows, rows, P(DP), P(DP), P()),
        out_specs=(rows, rows, rows, rows, P(("y", "c") + DP, None)),
        check_vma=False,
    )
```

```python
import functools
import math

import jax
import jax.numpy as jnp
from jax import lax
from jax.experimental import pallas as pl
from jax.experimental.pallas import tpu as pltpu
from jax.sharding import Mesh
from jax.sharding import PartitionSpec as P

HD = 128
RUN = 8
X_SIZE = 4
Z_LOW = 4
MAX_RUNS = 64
STEP_RUNS = 16
BRING = 4
PACK_COLUMNS = 1024
LOG2_E = math.log2(math.e)
SERVER_HEADS = 4
TAG_ROWS = 16
NEG_FILL = -1e30
F32 = jnp.float32
BF16 = jnp.bfloat16
NT = (((1,), (1,)), ((), ()))
TN = (((0,), (0,)), ((), ()))
DP = ("zh", "zl", "x")


def whole(memory=pltpu.VMEM):
    return pl.BlockSpec(memory_space=memory)


def params(limit):
    return pltpu.CompilerParams(vmem_limit_bytes=limit * 1024 * 1024)


def slot_row(doc, servers):
    tokens, docs = doc.shape[1], servers.shape[1]
    same = lax.broadcasted_iota(jnp.int32, (docs, tokens), 0) == doc
    names = jnp.broadcast_to(servers.astype(F32), (RUN, docs)).astype(BF16)
    server = jnp.dot(names, same.astype(F32).astype(BF16), preferred_element_type=F32)[:1].astype(jnp.int32)
    return server * RUN + lax.broadcasted_iota(jnp.int32, (1, tokens), 1) % RUN


def one_hot(slots, slot):
    return (lax.broadcasted_iota(jnp.int32, (slots, slot.shape[1]), 0) == slot).astype(F32).astype(BF16)


def pack_kernel(
    doc_hbm, offset_hbm, servers_hbm, query_hbm, grad_hbm, key_hbm, value_hbm, out_hbm, pairs_ref, slot_ref,
    doc_ref, offset_ref, servers_ref, query_ref, grad_ref, key_ref, value_ref, out_ref, in_sems, out_sems,
):
    slots, tokens = out_ref.shape[0], doc_ref.shape[1]
    sources = (doc_hbm, offset_hbm, servers_hbm, query_hbm, grad_hbm, key_hbm, value_hbm)
    targets = (doc_ref, offset_ref, servers_ref, query_ref, grad_ref, key_ref, value_ref)
    arrivals = [pltpu.make_async_copy(a, b, in_sems.at[i]) for i, (a, b) in enumerate(zip(sources, targets))]
    for copy in arrivals:
        copy.start()
    for copy in arrivals[:3]:
        copy.wait()
    doc = doc_ref[...]
    slot = slot_row(doc, servers_ref[...])
    slot_ref[...] = jnp.broadcast_to(slot, slot_ref.shape)
    hot = one_hot(slots, slot)
    place = offset_ref[...] // RUN
    line = lax.broadcasted_iota(jnp.int32, (HD, tokens), 0)
    tags = jnp.where(line == 0, doc + 1, jnp.where(line == 1, place, 0)).astype(F32).astype(BF16)
    tags = lax.dot_general(hot, tags, NT, preferred_element_type=F32).astype(BF16)
    departures = []

    def send(begin, end):
        columns = pl.ds(begin, end - begin)
        copy = pltpu.make_async_copy(out_ref.at[:, columns], out_hbm.at[:, columns], out_sems.at[len(departures)])
        copy.start()
        departures.append(copy)

    at = 0
    for copy, ref in zip(arrivals[3:], targets[3:]):
        copy.wait()
        width = ref.shape[1]
        part = min(width, PACK_COLUMNS)
        for begin in range(0, width, part):
            rows = jnp.dot(hot, ref[:, begin : begin + part], preferred_element_type=F32).astype(BF16)
            out_ref[:, at : at + part] = rows
            at += part
            if width > HD:
                send(at - part, at)
    out_ref[:, at : at + HD] = tags
    send(at - 2 * HD, at + HD)
    pairs_ref[:tokens, :HD] = key_ref[...]
    pairs_ref[:tokens, HD:] = value_ref[...]
    line = lax.broadcasted_iota(jnp.int32, (TAG_ROWS, tokens), 0)
    tags = jnp.where(line == 0, doc, jnp.where(line == 1, place, 0)).astype(F32).astype(BF16)
    pairs_ref[tokens:, :] = jnp.zeros((TAG_ROWS, 2 * HD), BF16)
    pairs_ref[tokens:, :tokens] = tags
    for copy in departures:
        copy.wait()


def turn_kernel(z_high, z_low, me_ref, layer_hbm, *refs):
    outs, layer_ref, sem = refs[:X_SIZE], refs[X_SIZE], refs[X_SIZE + 1]
    copy = pltpu.make_async_copy(layer_hbm, layer_ref, sem)
    copy.start()
    width = layer_ref.shape[1]
    rows = width // X_SIZE
    deep = rows // (z_high * z_low)
    new = lax.broadcasted_iota(jnp.int32, (rows, width), 0)
    old = lax.broadcasted_iota(jnp.int32, (rows, width), 1)
    ahead = old - (new // deep * (X_SIZE * deep) + new % deep)
    copy.wait()
    for d in range(X_SIZE):
        hot = (ahead == (me_ref[0] + d) % X_SIZE * deep).astype(F32).astype(BF16)
        outs[d][...] = lax.dot_general(hot, layer_ref[...], NT, preferred_element_type=F32).astype(BF16)


def server_kernel(tag_ref, query_ref, grad_ref, key_ref, value_ref, out_ref, bias, key_acc, value_acc):
    head = pl.program_id(0)

    @pl.when(head == 0)
    def _():
        slots = tag_ref.shape[0]
        tags = tag_ref[...].astype(F32)
        turned = tags.T
        col_doc, row_doc = tags[:, 0:1], turned[0:1, :]
        col_pos = tags[:, 1:2] * RUN + (lax.broadcasted_iota(jnp.int32, (slots, 1), 0) % RUN).astype(F32)
        row_pos = turned[1:2, :] * RUN + (lax.broadcasted_iota(jnp.int32, (1, slots), 1) % RUN).astype(F32)
        bias[...] = jnp.where((col_doc == row_doc) & (col_pos <= row_pos), 0.0, NEG_FILL)
        key_acc[...] = jnp.zeros_like(key_acc)
        value_acc[...] = jnp.zeros_like(value_acc)

    scale = float(HD) ** (-0.5)
    key, value = key_ref[...], value_ref[...]
    heads = range(query_ref.shape[1] // HD)
    cut = lambda ref: [ref[:, h * HD : (h + 1) * HD] for h in heads]
    query, grad = cut(query_ref), cut(grad_ref)
    scores = [lax.dot_general(key, query[h], NT, preferred_element_type=F32) + bias[...] for h in heads]
    grad_weights = [lax.dot_general(value, grad[h], NT, preferred_element_type=F32) for h in heads]
    key_part, value_part = key_acc[...], value_acc[...]
    for h in heads:
        top = jnp.max(scores[h], axis=0, keepdims=True)
        exp_scores = jnp.exp2((scores[h] - top) * (scale * LOG2_E))
        total = jnp.sum(exp_scores, axis=0, keepdims=True)
        weights = exp_scores * (1.0 / total)
        weights_low = weights.astype(BF16)
        row_delta = jnp.sum(weights_low.astype(F32) * grad_weights[h], axis=0, keepdims=True)
        grad_scores = (weights * (grad_weights[h] - row_delta)).astype(BF16)
        value_part += jnp.dot(weights_low, grad[h], preferred_element_type=F32)
        key_part += jnp.dot(grad_scores, query[h], preferred_element_type=F32)
    key_acc[...] = key_part
    value_acc[...] = value_part

    @pl.when(head == pl.num_programs(0) - 1)
    def _():
        out_ref[:, :HD] = (key_acc[...] * scale).astype(BF16)
        out_ref[:, HD:] = value_acc[...].astype(BF16)


def home_kernel(
    group, unroll, place_ref, reach_ref, query_hbm, grad_hbm, pairs_ref, mixed_ref, query_grad_ref,
    rows, query_ref, grad_ref, query, grad, mixed, query_grad, sems,
):
    scale = float(HD) ** (-0.5)
    count = query_ref.shape[0] // RUN
    arrivals = [
        pltpu.make_async_copy(query_hbm, query_ref, sems.at[0]),
        pltpu.make_async_copy(grad_hbm, grad_ref, sems.at[1]),
    ]
    for copy in arrivals:
        copy.start()
    rows[...] = jnp.zeros_like(rows)
    for copy in arrivals:
        copy.wait()
    query[...] = query_ref[...].astype(F32)
    grad[...] = grad_ref[...].astype(F32)

    def stack(ref, run):
        parts = [ref[pl.ds(pl.multiple_of(run * RUN, RUN), RUN), h * HD : (h + 1) * HD] for h in range(group)]
        return jnp.concatenate(parts, axis=0)

    def unstack(ref, run, block):
        for h in range(group):
            ref[pl.ds(pl.multiple_of(run * RUN, RUN), RUN), h * HD : (h + 1) * HD] = block[h * RUN : (h + 1) * RUN]

    def bring(u, run):
        def several(i, carry):
            for j in range(BRING):
                k = i * BRING + j
                place = place_ref[run, k]
                two = pairs_ref[pl.ds(pl.multiple_of(place // 2 * (2 * RUN), 2 * RUN), 2 * RUN), :].astype(F32)
                one = jnp.where(place % 2 == 1, two[RUN:], two[:RUN])
                rows[u, pl.ds(pl.multiple_of(k * RUN, RUN), RUN), :] = one
            return carry

        lax.fori_loop(0, reach_ref[run] // BRING + 1, several, 0)

    def part(index, reach_runs):
        reach_rows = reach_runs * RUN
        for u in range(unroll):
            bring(u, index * unroll + u)
        rows_each = group * RUN
        token = lax.broadcasted_iota(jnp.int32, (rows_each, reach_rows), 0) % RUN
        ahead = lax.broadcasted_iota(jnp.int32, (rows_each, reach_rows), 1) - token
        each = range(unroll)
        cut = lambda block: [block[u * rows_each : (u + 1) * rows_each] for u in each]
        runs = [index * unroll + u for u in each]
        blocks = [rows[u, :reach_rows].astype(BF16) for u in each]
        keys, values = [block[:, :HD] for block in blocks], [block[:, HD:] for block in blocks]
        query_runs = [stack(query, run).astype(BF16) for run in runs]
        grad_full = jnp.concatenate([stack(grad, run) for run in runs], axis=0)
        grad_runs = cut(grad_full.astype(BF16))
        dots = lambda left, right: [lax.dot_general(left[u], right[u], NT, preferred_element_type=F32) for u in each]
        scores = dots(query_runs, keys)
        scores = [jnp.where(ahead <= reach_ref[runs[u]] * RUN, scores[u], NEG_FILL) for u in each]
        scores = jnp.concatenate(scores, axis=0)
        grad_weights = jnp.concatenate(dots(grad_runs, values), axis=0)
        top = jnp.max(scores, axis=1, keepdims=True)
        exp_scores = jnp.exp((scores - top) * scale)
        total = jnp.sum(exp_scores, axis=1, keepdims=True)
        weights = exp_scores * (1.0 / total)
        low = cut(weights.astype(BF16))
        mixed_full = [jnp.dot(low[u], values[u], preferred_element_type=F32) for u in each]
        row_delta = jnp.sum(grad_full * jnp.concatenate(mixed_full, axis=0), axis=1, keepdims=True)
        grad_scores = cut((weights * (grad_weights - row_delta)).astype(BF16))
        back = [jnp.dot(grad_scores[u], keys[u], preferred_element_type=F32) * scale for u in each]
        for u in each:
            unstack(mixed, runs[u], mixed_full[u])
            unstack(query_grad, runs[u], back[u])

    def step(index, carry):
        reach = reach_ref[index * unroll]
        for u in range(1, unroll):
            reach = jnp.maximum(reach, reach_ref[index * unroll + u])
        below = 0
        for reach_runs in (STEP_RUNS, 2 * STEP_RUNS, MAX_RUNS):
            pl.when((reach >= below) & (reach < reach_runs))(functools.partial(part, index, reach_runs))
            below = reach_runs
        return carry

    lax.fori_loop(0, count // unroll, step, 0)
    mixed_ref[...] = mixed[...].astype(BF16)
    query_grad_ref[...] = query_grad[...].astype(BF16)


def own_kernel(slot_ref, back_ref, key_grad_ref, value_grad_ref, near_ref):
    hot = one_hot(back_ref.shape[0], slot_ref[:1])
    rows = lax.dot_general(hot, back_ref[...], TN, preferred_element_type=F32).astype(BF16)
    key_grad_ref[...] = rows[:, :HD]
    value_grad_ref[...] = rows[:, HD:]
    for i in range(near_ref.shape[0]):
        near_ref[i] = rows[:, HD:]


def weight_kernel(x_ref, core_ref, *refs):
    layers, own_ref, other_ref, out_ref = refs[:X_SIZE], refs[X_SIZE], refs[X_SIZE + 1], refs[X_SIZE + 2]
    me, core = x_ref[0], core_ref[0]
    y_size = own_ref.shape[0] // X_SIZE
    layer = jnp.concatenate([ref[...] for ref in layers], axis=1)
    for y in range(y_size):
        parts = []
        for d in range(X_SIZE):
            at = (me - d + X_SIZE) % X_SIZE * y_size + y
            own, other = own_ref[at], other_ref[at]
            parts.append(jnp.concatenate([jnp.where(core == 0, own, other), jnp.where(core == 0, other, own)], axis=1))
        total = jnp.dot(layer, jnp.concatenate(parts, axis=0), preferred_element_type=F32)
        out_ref[:, 2 * y * HD : 2 * (y + 1) * HD] = total.astype(BF16)


def exact_pick(left, right):
    return lax.dot_general(left.astype(BF16), right.astype(BF16), NT, preferred_element_type=F32).astype(jnp.int32)


def shards(query_rows, key_rows, value_rows, output_grad, layer_input, token_document, token_offset, document_server):
    dp_size = lax.axis_size(DP)
    high, low = lax.axis_size("zh"), lax.axis_size("zl")
    tokens = query_rows.shape[0]
    runs = tokens // RUN
    slots = dp_size * RUN
    width = query_rows.shape[1]
    group = width // HD
    doc, offset, servers = token_document[None, :], token_offset[None, :], document_server[None, :]
    x_index, core = lax.axis_index("x").astype(jnp.int32), lax.axis_index("c").astype(jnp.int32)
    x_index, core = x_index.reshape(1), core.reshape(1)

    def call(kernel, out_shape, *args, **more):
        shapes = [jax.ShapeDtypeStruct(shape, BF16) if isinstance(shape, tuple) else shape for shape in out_shape]
        out = pl.pallas_call(
            kernel,
            out_shape=shapes,
            in_specs=more.pop("in_specs", [whole()] * len(args)),
            out_specs=more.pop("out_specs", [whole()] * len(shapes)),
            compiler_params=params(more.pop("limit", 32)),
            **more,
        )(*args)
        return out[0] if len(shapes) == 1 else list(out)

    def swap(block, axis):
        return lax.all_to_all(block, axis, split_axis=0, concat_axis=0, tiled=True)

    sent, pairs, slot = call(
        pack_kernel,
        [(slots, 2 * width + 3 * HD), (tokens + TAG_ROWS, 2 * HD), jax.ShapeDtypeStruct((RUN, tokens), jnp.int32)],
        doc, offset, servers, query_rows, output_grad, key_rows, value_rows,
        in_specs=[whole(pltpu.HBM)] * 7,
        out_specs=[whole(pltpu.HBM), whole(), whole()],
        scratch_shapes=[pltpu.VMEM((1, tokens), jnp.int32)] * 2 + [pltpu.VMEM(servers.shape, jnp.int32)]
        + [pltpu.VMEM((tokens, width), BF16)] * 2 + [pltpu.VMEM((tokens, HD), BF16)] * 2
        + [pltpu.VMEM((slots, 2 * width + 3 * HD), BF16), pltpu.SemaphoreType.DMA((7,)), pltpu.SemaphoreType.DMA((2 * width // PACK_COLUMNS + 1,))],
        limit=60,
        name="pack",
    )
    part = width // X_SIZE
    sent, layer_input, pairs = lax.optimization_barrier((sent, layer_input, pairs))
    arrived = swap(sent.reshape(dp_size, RUN, -1), DP)
    turned = call(
        functools.partial(turn_kernel, high, low), [(part, tokens)] * X_SIZE, x_index, layer_input,
        in_specs=[whole(pltpu.SMEM), whole(pltpu.HBM)],
        scratch_shapes=[pltpu.VMEM((tokens, width), BF16), pltpu.SemaphoreType.DMA],
        limit=60,
        name="turn",
    )
    all_pairs = lax.all_gather(pairs, DP, axis=0, tiled=True)
    layers = [turned[0]] + [
        lax.ppermute(turned[d], "x", [(i, (i + d) % X_SIZE) for i in range(X_SIZE)]) for d in range(1, X_SIZE)
    ]
    arrived, *layers = lax.optimization_barrier((arrived, *layers))
    arrived = arrived.reshape(slots, -1)

    steps = group // SERVER_HEADS
    column = lambda at: pl.BlockSpec((slots, SERVER_HEADS * HD), lambda h, at=at: (0, at + h))
    fixed = lambda at: pl.BlockSpec((slots, HD), lambda h, at=at: (0, at))
    served = call(
        server_kernel, [(slots, 2 * HD)], *[arrived] * 5,
        grid=(steps,),
        in_specs=[fixed(2 * group + 2), column(0), column(steps), fixed(2 * group), fixed(2 * group + 1)],
        out_specs=[pl.BlockSpec((slots, 2 * HD), lambda h: (0, 0))],
        scratch_shapes=[pltpu.VMEM((slots, slots), F32), pltpu.VMEM((slots, HD), F32), pltpu.VMEM((slots, HD), F32)],
        name="server",
    )

    back = swap(served.reshape(dp_size, RUN, -1), DP).reshape(slots, -1)
    key_grad, value_grad, near = call(
        own_kernel, [(tokens, HD), (tokens, HD), (X_SIZE * lax.axis_size("y"), tokens, HD)], slot, back, name="own"
    )

    y_size = lax.axis_size("y")
    own_core = swap(near, ("x", "y"))
    other_core = lax.ppermute(own_core, "c", [(0, 1), (1, 0)])
    channels = 2 * y_size * HD
    plane = call(
        weight_kernel, [(part, channels)], x_index, core, *layers, own_core, other_core,
        in_specs=[whole(pltpu.SMEM)] * 2 + [whole()] * (X_SIZE + 2), name="weight",
    )
    plane, all_pairs = lax.optimization_barrier((plane, all_pairs))
    block = swap(plane.reshape(high * low, part // (high * low), channels), ("zh", "zl"))
    weight_grad = jnp.sum(block.astype(F32), axis=0) * (1.0 / math.sqrt(tokens * dp_size))

    tags = all_pairs.reshape(dp_size, tokens + TAG_ROWS, 2 * HD)[:, tokens : tokens + 2, :tokens:RUN]
    all_doc, all_place = tags[:, 0].reshape(1, -1), tags[:, 1].reshape(1, -1)
    run_doc, run_place = token_document[::RUN], token_offset[::RUN] // RUN
    same = run_doc.astype(BF16)[:, None] == all_doc
    at = jnp.arange(MAX_RUNS, dtype=jnp.int32).astype(BF16)[:, None] == all_place
    ids = jnp.arange(dp_size * runs, dtype=jnp.int32)[None, :]
    device, run = exact_pick(same, jnp.where(at, ids // runs, 0)), exact_pick(same, jnp.where(at, ids % runs, 0))
    place = device * (runs + TAG_ROWS // RUN) + run
    unroll = 8
    wide = (tokens, width)
    attended, query_grad = call(
        functools.partial(home_kernel, group, unroll), [wide, wide],
        place, run_place, query_rows, output_grad, all_pairs,
        in_specs=[whole(pltpu.SMEM), whole(pltpu.SMEM), whole(pltpu.HBM), whole(pltpu.HBM), whole()],
        scratch_shapes=[pltpu.VMEM((unroll, MAX_RUNS * RUN, 2 * HD), F32)] + [pltpu.VMEM(wide, BF16)] * 2
        + [pltpu.VMEM(wide, F32)] * 4 + [pltpu.SemaphoreType.DMA((2,))],
        limit=60,
        name="home",
    )
    return (attended, query_grad, key_grad, value_grad, weight_grad)


def solution(mesh):
    shape = (-1, Z_LOW, X_SIZE, mesh.shape["tensor"] // 2, 2)
    fine = Mesh(mesh.devices.reshape(shape), ("zh", "zl", "x", "y", "c"))
    rows = P(DP, ("y", "c"))
    return jax.shard_map(
        shards,
        mesh=fine,
        in_specs=(rows, rows, rows, rows, rows, P(DP), P(DP), P()),
        out_specs=(rows, rows, rows, rows, P(("y", "c") + DP, None)),
        check_vma=False,
    )
```
